256 devices in a mesh: attn: 16 (over y, x), expert: 8 (over z), tp: 2 (over core).
Axes of the slice: x: 4, y: 4, z: 8, core: 2. Of those that a mesh axis runs over, the one named last changes fastest.
Arguments:
- tokens: bfloat16 [32, 6144], P('expert', 'attn'), may hold values from -6 to 6
- queries: bfloat16 [32, 48, 128], P(('attn', 'tp'), 'expert'), may hold values from -120 to 120
- key_cache: bfloat16 [32, 8, 4096, 128], P(('attn', 'tp'), 'expert'), may hold values from -6 to 6
- value_cache: bfloat16 [32, 8, 4096, 128], P(('attn', 'tp'), 'expert'), may hold values from -6 to 6
- lengths: int32 [32], P(('attn', 'tp')), may hold values from 2 to 4096, as said below
- out_weight: bfloat16 [6144, 6144], P('expert', 'attn'), may hold values from -1.75 to 1.75
- norm_gain: bfloat16 [6144], P('attn'), may hold values from 0.099609375 to 1.8984375
- router_weight: float32 [6144, 8], P('attn'), may hold values from -0.15625 to 0.15625
- routes: int32 [32, 2], P('expert'), may hold values from 0 to 7, all different within a row; in each aligned block of 4 rows (0 to 3, 4 to 7, ...) at most 3 rows name the same one
- up_weight: bfloat16 [8, 6144, 2, 8192], P('expert', None, None, ('attn', 'tp')), may hold values from -0.078125 to 0.078125
- down_weight: bfloat16 [8, 8192, 6144], P('expert', ('attn', 'tp')), may hold values from -0.0625 to 0.0625
Outputs:
- mixed: bfloat16 [32, 6144], P('expert', 'attn')
The draws below stay inside these ranges and needn't reach their ends.
Inputs may be any that keep to these rules, and one draw needn't show every extreme that they name: Row r's live slots are 0 to lengths[r] - 1; some row has all 4096 slots live. `routes`: the two experts of a row differ; within the rows of one index of expert no expert is named by more than 3 rows, a bound that some block reaches.
All inputs are finite; a program needn't handle non-finite values.
Results may differ from the reference program's by a relative error of at most 0.02.
Values may be sent and summed in bfloat16 or wider, within the bound.
A program may use at most 64 MiB of HBM per device.

```python
import math
import jax
import jax.numpy as jnp
import numpy as np
from jax import lax

D = 6144
HQ = 48
KVH = 8
HD = 128
TOP = 2
FFW = 8192
CACHE = 4096
EXPERTS = 8
ROWS = 32
ROW_BLK = 4
CAP = 3
N_ATTN = 16
N_TP = 2


def cache_keys(key):
    return jnp.clip(jax.random.normal(key, (ROWS, KVH, CACHE, HD), jnp.float32), -6.0, 6.0)


def draw_key_cache(key, part):
    base = cache_keys(key)
    return base.astype(jnp.bfloat16)


def draw_queries(key, part):
    key = jax.random.fold_in(key, 12)
    drawn = jnp.clip(jax.random.normal(key, (ROWS, HQ, HD), jnp.float32), -6.0, 6.0)
    return drawn.astype(jnp.bfloat16)


def draw_lengths(key, part):
    key = jax.random.fold_in(key, 13)
    first, second = jax.random.split(key)
    spans = jax.random.randint(first, (ROWS,), 2, CACHE + 1)
    chosen = jax.random.randint(second, (), 0, ROWS)
    return jnp.where(jnp.arange(ROWS) == chosen, CACHE, spans).astype(jnp.int32)


def level_of(own_key, dims, pieces, low, high):
    loudness = 1.0
    for dim, shards_of in pieces:
        steps = jax.random.uniform(jax.random.fold_in(jax.random.fold_in(own_key, 6), dim), (shards_of,), jnp.float32, low / len(pieces), high / len(pieces))
        loudness = loudness * jnp.repeat(jnp.exp(steps), dims[dim] // shards_of).reshape((-1,) + (1,) * (len(dims) - 1 - dim))
    return loudness


def shared_out(own_key, own, number, rows, count, top, most, slope):
    order = jax.random.permutation(own_key, count)
    packed, common = portions_of(count, rows * top, most, slope, True), portions_of(count, rows * top, most, slope, False)
    places = jnp.arange(count)

    def named(tallies, turn):
        used = int((tallies > 0).sum())
        fixed = max(1, used // 4)
        moved = fixed + (places - fixed + turn * (used - fixed)) % max(1, count - fixed)
        return jnp.zeros((count,), jnp.int32).at[order[jnp.where(places < fixed, places, moved)]].set(jnp.asarray(tallies, jnp.int32))

    tallies = jnp.where(number % 4 == 0, named(packed, number // 4), named(common, number - number // 4 - 1))
    mixed = jax.random.permutation(jax.random.fold_in(own, 3), count)
    giver, sink = mixed[0:count // 2 * 2:2], mixed[1:count // 2 * 2:2]
    slack = jnp.minimum(tallies[giver] - 1, most - tallies[sink]) // 2
    slack = jnp.where((giver == order[0]) | (sink == order[0]) | (tallies[sink] == 0), 0, jnp.maximum(slack, 0))
    moved = jax.random.randint(jax.random.fold_in(own, 4), (count // 2,), 0, 1 << 20) % (slack + 1)
    tallies = tallies.at[giver].add(-moved).at[sink].add(moved)
    members = jnp.searchsorted(jnp.cumsum(tallies), jnp.arange(rows * top), side="right").astype(jnp.int32)
    table = members.reshape(top, rows).T
    table = table[jax.random.permutation(jax.random.fold_in(own, 1), rows)]
    turn = jax.random.randint(jax.random.fold_in(own, 2), (rows, 1), 0, top)
    return jnp.take_along_axis(table, (jnp.arange(top)[None, :] + turn) % top, axis=1)


def portions_of(amount, total, most, skew, full):
    portions = [(1 << 20) // math.isqrt(standing ** skew) + 1 for standing in range(1, amount + 1)]
    largest = most if full else min(most, max(-(-total // amount), total * portions[0] // sum(portions)))
    least = 1 if total - largest >= amount - 1 else 0
    holding, surplus = [largest] + [least] * (amount - 1), total - largest - least * (amount - 1)
    while surplus > 0:
        free = [i for i in range(1, amount) if holding[i] < largest] or [i for i in range(1, amount) if holding[i] < most]
        pool, budget = sum([portions[i] for i in free]), surplus
        for i in free:
            more = min(most - holding[i], max(1, budget * portions[i] // pool), surplus)
            holding[i] = holding[i] + more
            surplus = surplus - more
    return np.array(holding)


def noise(own_key, extent, spread, most, pieces=(), kind=jnp.bfloat16):
    entries = spread * jax.random.normal(own_key, extent, jnp.float32)
    if pieces:
        entries = entries * level_of(own_key, extent, pieces, -0.22, 0.18)
    return jnp.clip(entries, -most, most).astype(kind)


def setup_inputs(seed: int = 0) -> dict:
    streams_of = jax.random.split(jax.random.key(seed), 12)
    tokens = noise(streams_of[0], (ROWS, D), 1.0, 6.0, ((0, 8), (1, 16)))
    queries = draw_queries(jax.random.fold_in(streams_of[11], 71), 0)
    key_cache = draw_key_cache(jax.random.fold_in(streams_of[11], 71), 0)
    value_cache = noise(streams_of[3], (ROWS, KVH, CACHE, HD), 1.0, 6.0, ((0, 32), (1, 8)))
    lengths = draw_lengths(jax.random.fold_in(streams_of[11], 71), 0)
    out_weight = noise(streams_of[5], (HQ * HD, D), (max(1, HQ * HD // 512)) ** -0.5, 1.75, ((0, 8), (1, 16)))
    norm_gain = jnp.clip(1.0 + 0.18 * jax.random.normal(streams_of[6], (D,), jnp.float32), 0.099609375, 1.8984375).astype(jnp.bfloat16)
    router_weight = noise(streams_of[7], (D, EXPERTS), (D // 4) ** -0.5, 0.15625, ((0, 16),), jnp.float32)
    routes_keys = jax.random.split(jax.random.fold_in(streams_of[8], 1), ROWS // ROW_BLK)
    routes_turns = jax.random.permutation(jax.random.fold_in(streams_of[8], 3), ROWS // ROW_BLK)
    routes = jax.vmap(lambda own, number: shared_out(jax.random.fold_in(streams_of[8], 2), own, number, ROW_BLK, EXPERTS, TOP, CAP, 2))(routes_keys, routes_turns).reshape((ROWS, TOP))
    up_weight = noise(streams_of[9], (EXPERTS, D, 2, FFW), D ** -0.5, 0.078125, ((0, 8), (3, 32)))
    down_weight = noise(streams_of[10], (EXPERTS, FFW, D), FFW ** -0.5, 0.0625, ((0, 8), (1, 32)))
    return {"tokens": tokens, "queries": queries, "key_cache": key_cache, "value_cache": value_cache, "lengths": lengths, "out_weight": out_weight, "norm_gain": norm_gain, "router_weight": router_weight, "routes": routes, "up_weight": up_weight, "down_weight": down_weight}


def attend_row(query, keys, values, length):
    group = query.shape[0] // keys.shape[0]
    grouped = query.astype(jnp.float32).reshape(keys.shape[0], group, keys.shape[2])
    scores = jnp.einsum('kgd,ktd->kgt', grouped, keys.astype(jnp.float32)) * keys.shape[2] ** (-0.5)
    live = jnp.arange(keys.shape[1]) < length
    scores = jnp.where(live[None, None, :], scores, -jnp.inf)
    top = lax.optimization_barrier(jnp.max(scores, axis=2, keepdims=True))
    weights = jnp.exp(scores - top)
    total = lax.optimization_barrier(jnp.sum(weights, axis=2, keepdims=True))
    probs = (weights / total).astype(jnp.bfloat16)
    mixed = jnp.einsum('kgt,ktd->kgd', probs.astype(jnp.float32), values.astype(jnp.float32))
    return mixed.reshape(-1).astype(jnp.bfloat16)

def expert_rows(normed, up_weight, down_weight):
    blocks = N_ATTN * N_TP

    def single(weights):
        w_up, w_down = weights
        both = jnp.einsum('rd,dcf->rcf', normed.astype(jnp.float32), w_up.astype(jnp.float32))
        hidden = (jax.nn.silu(both[:, 0]) * both[:, 1]).astype(jnp.bfloat16)
        hidden_blocks = hidden.astype(jnp.float32).reshape(hidden.shape[0], blocks, -1)
        down_blocks = w_down.astype(jnp.float32).reshape(blocks, -1, w_down.shape[1])
        parts = jnp.einsum('rbf,bfd->brd', hidden_blocks, down_blocks).astype(jnp.bfloat16)
        parts = lax.optimization_barrier(parts)
        return lax.optimization_barrier(jnp.sum(parts.astype(jnp.float32), axis=0)).astype(jnp.bfloat16)
    return lax.map(single, (up_weight, down_weight))

def reference(tokens, queries, key_cache, value_cache, lengths, out_weight, norm_gain, router_weight, routes, up_weight, down_weight):
    heads = lax.map(lambda item: attend_row(item[0], item[1], item[2], item[3]), (queries, key_cache, value_cache, lengths))
    attended = jnp.dot(heads, out_weight, preferred_element_type=jnp.float32)
    resid = lax.optimization_barrier((tokens.astype(jnp.float32) + attended).astype(jnp.bfloat16))
    wide = resid.astype(jnp.float32)
    scale = lax.rsqrt(lax.optimization_barrier(jnp.sum(wide * wide, axis=1, keepdims=True)) / D + 1e-05)
    gained = wide * norm_gain.astype(jnp.float32)
    normed = (gained * scale).astype(jnp.bfloat16)
    logits = jnp.dot(gained, router_weight, precision=lax.Precision.HIGHEST) * scale
    chosen = jnp.take_along_axis(logits, routes, axis=1)
    gates = jax.nn.sigmoid(jnp.stack([chosen[:, 0] - chosen[:, 1], chosen[:, 1] - chosen[:, 0]], axis=1))
    outputs = expert_rows(normed, up_weight, down_weight)
    row_index = jnp.arange(ROWS).astype(jnp.int32)[:, None]
    picked = outputs[routes, row_index]
    moe = lax.optimization_barrier(jnp.sum(gates[:, :, None] * picked.astype(jnp.float32), axis=1))
    return (wide + moe).astype(jnp.bfloat16)
```

```python
import jax
import jax.numpy as jnp
from jax import lax
from jax.experimental import pallas as pl
from jax.experimental.pallas import tpu as pltpu
from jax.sharding import PartitionSpec as P

MESH = pl.DeviceIdType.MESH
F32, BF16 = jnp.float32, jnp.bfloat16
D = 6144
HD = 128
GROUP = 6
CACHE = 4096
NA, NE, NT = 16, 8, 2
HALF = 16
COLS = 384
HID = 256
NEAR = sorted(
    ((dy, dx) for dy in range(4) for dx in range(4)),
    key=lambda o: min(o[0], 4 - o[0]) + min(o[1], 4 - o[1]),
)


def drain(ref, sem):
    pltpu.make_async_copy(ref, ref, sem).wait()


def kernel(
    tok_hbm, q_hbm, k_hbm, v_hbm, len_ref, wo_hbm, gain_hbm, router_hbm, routes_hbm, up_hbm, down_hbm,
    out_ref,
    tok, q, k, v, wo, gain, router, routes, up, up2, down,
    heads, gath, zsum, resid, feats, stat, stats, stat_tot, hid, part, part_sib, reduced, back, ret_s, ret,
    in_sem, p1_s, p1_r, p2_s, p2_r, p3_s, p3_r, fw_s, fw_r, st_s, st_r, sib_s, sib_r, p4x_s, p4x_r, p4_s, p4_r, p5_s, p5_r,
):
    a, e, t = lax.axis_index("attn"), lax.axis_index("expert"), lax.axis_index("tp")
    ay, ax = lax.div(a, 4), lax.rem(a, 4)
    sib = (a, e, 1 - t)

    def near(o):
        return lax.rem(ay + o[0], 4) * 4 + lax.rem(ax + o[1], 4)

    loads = {}
    pairs = (
        ("q", q_hbm, q), ("k", k_hbm, k), ("v", v_hbm, v), ("wo", wo_hbm, wo), ("tok", tok_hbm, tok),
        ("gain", gain_hbm, gain), ("router", router_hbm, router), ("routes", routes_hbm, routes),
        ("up", up_hbm, up), ("down", down_hbm, down),
    )
    for n, (name, src, dst) in enumerate(pairs):
        loads[name] = pltpu.make_async_copy(src, dst, in_sem.at[n])
        loads[name].start()

    barrier = pltpu.get_barrier_semaphore()

    def greet_plane(j, c):
        other = lax.rem(2 * a + t + 1 + j, 32)
        pl.semaphore_signal(
            barrier, inc=1, device_id=(lax.div(other, 2), e, lax.rem(other, 2)), device_id_type=MESH
        )
        return c

    def greet_z(j, c):
        other = lax.rem(2 * e + t + 2 + j, 16)
        pl.semaphore_signal(
            barrier, inc=1, device_id=(a, lax.rem(e + 1 + lax.div(j, 2), NE), lax.rem(other, 2)), device_id_type=MESH
        )
        return c

    lax.fori_loop(0, 31, greet_plane, 0)
    lax.fori_loop(0, 14, greet_z, 0)

    loads["q"].wait()
    loads["k"].wait()
    scores = lax.dot_general(
        q[...], k[...], (((1,), (1,)), ((), ())), preferred_element_type=F32
    ) * (HD**-0.5)
    live = lax.broadcasted_iota(jnp.int32, scores.shape, 1) < len_ref[0]
    scores = jnp.where(live, scores, -jnp.inf)
    weights = jnp.exp(scores - jnp.max(scores, axis=1, keepdims=True))
    total = jnp.sum(weights, axis=1, keepdims=True)
    probs = (weights / total).astype(BF16)
    loads["v"].wait()
    mixed = jnp.dot(probs, v[...], preferred_element_type=F32)
    heads[...] = jnp.zeros_like(heads)
    heads[0:GROUP, :] = mixed

    pl.semaphore_wait(barrier, 45)

    half = lax.div(a, 8)
    slot = 2 * lax.rem(a, 8) + t

    def send_heads(o):
        pltpu.make_async_remote_copy(
            src_ref=heads, dst_ref=gath.at[slot], send_sem=p1_s, recv_sem=p1_r,
            device_id=(near(o), e, half), device_id_type=MESH,
        ).start()

    for o in NEAR[:0:-1]:
        send_heads(o)

    @pl.when(half != t)
    def _():
        send_heads((0, 0))

    @pl.when(half == t)
    def _():
        gath[slot] = heads[...]

    loads["up"].wait()

    def relayout(i, c):
        s = pl.ds(pl.multiple_of(i * COLS, COLS), COLS)
        up2[:, s, :] = jnp.swapaxes(up[s].astype(F32), 0, 1).astype(BF16)
        return c

    lax.fori_loop(0, D // COLS, relayout, 0)
    for name in ("wo", "tok", "gain", "router", "routes", "down"):
        loads[name].wait()
    mine = lax.broadcasted_iota(jnp.int32, (HALF, COLS), 0) // 4 == e - 4 * t
    tokens = jnp.where(mine, jnp.concatenate([tok[...].astype(F32)] * 4, axis=0), 0.0)

    @pl.when(half == t)
    def _():
        drain(gath.at[pl.ds(0, 15)], p1_r)

    @pl.when(half != t)
    def _():
        drain(gath, p1_r)

    flat = jnp.concatenate([gath[:, h, :].astype(BF16) for h in range(GROUP)], axis=1)
    projected = jnp.dot(flat, wo[...], preferred_element_type=F32) + tokens
    zsum[e] = projected.astype(BF16)

    for dz in (4, 3, 5, 2, 6, 1, 7):
        pltpu.make_async_remote_copy(
            src_ref=zsum.at[e], dst_ref=zsum.at[e], send_sem=p2_s, recv_sem=p2_r,
            device_id=(a, lax.rem(e + dz, NE), t), device_id_type=MESH,
        ).start()
    gains = gain[...].reshape(1, COLS).astype(F32)
    drain(zsum.at[pl.ds(0, 7)], p2_r)
    rounded = sum(zsum[i].astype(F32) for i in range(NE)).astype(BF16)
    wide = rounded.astype(F32)
    gained = wide * gains
    feats[a, t] = gained.astype(BF16)

    def feature_copy(o):
        return pltpu.make_async_remote_copy(
            src_ref=feats.at[a, t], dst_ref=feats.at[a, t], send_sem=p3_s, recv_sem=p3_r.at[a],
            device_id=(near(o), e, t), device_id_type=MESH,
        )

    def forward_copy(o):
        b = near(o)
        return pltpu.make_async_remote_copy(
            src_ref=feats.at[b, t], dst_ref=feats.at[b, t], send_sem=fw_s, recv_sem=fw_r.at[b],
            device_id=sib, device_id_type=MESH,
        )

    for o in NEAR[:0:-1]:
        feature_copy(o).start()
    forward_copy((0, 0)).start()
    resid[t] = rounded
    resid_copy = pltpu.make_async_remote_copy(
        src_ref=resid.at[t], dst_ref=resid.at[t], send_sem=sib_s.at[0], recv_sem=sib_r.at[0],
        device_id=sib, device_id_type=MESH,
    )
    resid_copy.start()

    lane = lax.broadcasted_iota(jnp.int32, (HALF, 128), 1)
    table = jnp.where(lane == 8, jnp.sum(wide * wide, axis=1, keepdims=True), 0.0)
    for x in range(NE):
        table = table + jnp.where(
            lane == x, jnp.sum(gained * router[x : x + 1, :], axis=1, keepdims=True), 0.0
        )
    stat[...] = table[0:8] + pltpu.roll(table[8:16], 64, 1)
    for o in NEAR[:0:-1]:
        pltpu.make_async_remote_copy(
            src_ref=stat, dst_ref=stats.at[a], send_sem=st_s, recv_sem=st_r,
            device_id=(near(o), e, t), device_id_type=MESH,
        ).start()
    stats[a] = stat[...]

    gate_acc = jnp.zeros((2 * HALF, HID), F32)
    up_acc = jnp.zeros((2 * HALF, HID), F32)

    def chunk(o, gate_acc, up_acc):
        b = near(o)
        drain(feats.at[b, 1 - t], fw_r.at[b])
        x = jnp.concatenate([feats[b, 0], feats[b, 1]], axis=0)
        s = pl.ds(pl.multiple_of(b * COLS, COLS), COLS)
        gate_acc = gate_acc + jnp.dot(x, up2[0, s, :], preferred_element_type=F32)
        up_acc = up_acc + jnp.dot(x, up2[1, s, :], preferred_element_type=F32)
        return gate_acc, up_acc

    LAG = 2
    for j, o in enumerate(NEAR):
        if j > 0:
            drain(feats.at[near(o), t], p3_r.at[near(o)])
            forward_copy(o).start()
        if j >= LAG:
            gate_acc, up_acc = chunk(NEAR[j - LAG], gate_acc, up_acc)
    drain(stats.at[pl.ds(0, 15)], st_r)
    stat_tot[t] = sum(stats[i] for i in range(NA))
    total_copy = pltpu.make_async_remote_copy(
        src_ref=stat_tot.at[t], dst_ref=stat_tot.at[t], send_sem=sib_s.at[1], recv_sem=sib_r.at[1],
        device_id=sib, device_id_type=MESH,
    )
    total_copy.start()
    for o in NEAR[NA - LAG :]:
        gate_acc, up_acc = chunk(o, gate_acc, up_acc)
    drain(stat_tot.at[1 - t], sib_r.at[1])
    tots = jnp.concatenate(
        [stat_tot[0], pltpu.roll(stat_tot[0], 64, 1), stat_tot[1], pltpu.roll(stat_tot[1], 64, 1)], axis=0
    )
    scale = lax.rsqrt(tots[:, 8:9] / D + 1e-05)
    gate_acc, up_acc = gate_acc * scale, up_acc * scale
    hidden = (gate_acc * jax.nn.sigmoid(gate_acc) * up_acc).astype(BF16)
    hid[...] = hidden

    def pair_copy(c):
        s = pl.ds(4 * c, 4)
        return pltpu.make_async_remote_copy(
            src_ref=part.at[1 - t, s], dst_ref=part_sib.at[s], send_sem=p4x_s, recv_sem=p4x_r.at[c],
            device_id=sib, device_id_type=MESH,
        )

    order = [lax.rem(ay + g, 4) for g in (2, 1, 3, 0)]
    for c in order:
        s = pl.ds(pl.multiple_of(c * (4 * COLS), 4 * COLS), 4 * COLS)
        d = jnp.dot(hid[...], down[:, s], preferred_element_type=F32).astype(BF16)
        for i in range(4):
            part[0, 4 * c + i] = d[0:HALF, i * COLS : (i + 1) * COLS]
            part[1, 4 * c + i] = d[HALF:, i * COLS : (i + 1) * COLS]
        pair_copy(c).start()
    for c in order:
        drain(part_sib.at[pl.ds(4 * c, 4)], p4x_r.at[c])
        for g in (2, 1, 3, 0):
            b = 4 * c + lax.rem(ax + g, 4)
            reduced[b] = (part[t, b].astype(F32) + part_sib[b].astype(F32)).astype(BF16)

            @pl.when(b != a)
            def _():
                pltpu.make_async_remote_copy(
                    src_ref=reduced.at[b], dst_ref=back.at[a], send_sem=p4_s, recv_sem=p4_r,
                    device_id=(b, e, t), device_id_type=MESH,
                ).start()

    back[a] = reduced[a]

    logits = tots * scale
    own = sum(jnp.where(e == i, logits[4 * i : 4 * i + 4], 0.0) for i in range(NE))
    square = (4, 128)
    lanes = lax.broadcasted_iota(jnp.int32, square, 1)
    rows = lax.broadcasted_iota(jnp.int32, (4, 4), 0)
    diag = lax.broadcasted_iota(jnp.int32, (4, 4), 1) == rows
    names = [
        jnp.sum(jnp.where(diag, jnp.broadcast_to(routes[n : n + 1, :], (4, 4)), 0), axis=1, keepdims=True)
        for n in range(2)
    ]
    chosen = [jnp.sum(jnp.where(lanes == names[n], own, 0.0), axis=1, keepdims=True) for n in range(2)]
    gates = [jax.nn.sigmoid(chosen[0] - chosen[1]), jax.nn.sigmoid(chosen[1] - chosen[0])]
    drain(resid.at[1 - t], sib_r.at[0])
    base = jnp.zeros((4, COLS), F32)
    for h in range(2):
        both = resid[h].astype(F32)
        for i in range(4):
            base = base + jnp.where(e == 4 * h + i, both[4 * i : 4 * i + 4], 0.0)

    drain(back.at[pl.ds(0, 15)], p4_r)
    summed = sum(back[i].astype(F32) for i in range(NA))

    for i in range(4):
        ret_s[i] = summed[4 * i : 4 * i + 4]
    for i in range(4):
        for other in range(2):
            row_owner = 4 * t + i
            itself = jnp.logical_and(row_owner == e, other == t)

            @pl.when(jnp.logical_not(itself))
            def _():
                pltpu.make_async_remote_copy(
                    src_ref=ret_s.at[i], dst_ref=ret.at[e], send_sem=p5_s, recv_sem=p5_r,
                    device_id=(a, row_owner, other), device_id_type=MESH,
                ).start()

            @pl.when(itself)
            def _():
                ret[e] = ret_s[i]

    home = lax.div(e, 4) == t

    @pl.when(home)
    def _():
        drain(ret.at[pl.ds(0, 7)], p5_r)
        drain(ret.at[pl.ds(0, 7)], p5_s)

    @pl.when(jnp.logical_not(home))
    def _():
        drain(ret, p5_r)
        drain(ret, p5_s)

    for x in range(NE):
        share = sum(jnp.where(names[n] == x, gates[n], 0.0) for n in range(2))
        base = base + share * ret[x]
    out_ref[...] = base.astype(BF16)

    @pl.when(half == t)
    def _():
        drain(gath.at[pl.ds(0, 15)], p1_s)

    @pl.when(half != t)
    def _():
        drain(gath, p1_s)

    drain(zsum.at[pl.ds(0, 7)], p2_s)
    drain(back.at[pl.ds(0, 15)], p3_s)
    drain(back, fw_s)
    drain(stats.at[pl.ds(0, 15)], st_s)
    drain(resid.at[t], sib_s.at[0])
    drain(stat_tot.at[t], sib_s.at[1])
    drain(part_sib, p4x_s)
    drain(back.at[pl.ds(0, 15)], p4_s)


def shards(
    tokens, queries, key_cache, value_cache, lengths, out_weight, norm_gain, router_weight, routes, up_weight, down_weight
):
    hbm = pl.BlockSpec(memory_space=pl.ANY)
    dma = pltpu.SemaphoreType.DMA
    return pl.pallas_call(
        kernel,
        out_shape=jax.ShapeDtypeStruct((4, COLS), BF16),
        in_specs=[hbm] * 4 + [pl.BlockSpec(memory_space=pltpu.SMEM)] + [hbm] * 6,
        out_specs=pl.BlockSpec(memory_space=pltpu.VMEM),
        scratch_shapes=[
            pltpu.VMEM((4, COLS), BF16),
            pltpu.VMEM((GROUP, HD), BF16),
            pltpu.VMEM((CACHE, HD), BF16),
            pltpu.VMEM((CACHE, HD), BF16),
            pltpu.VMEM((GROUP * HD, COLS), BF16),
            pltpu.VMEM((COLS,), BF16),
            pltpu.VMEM((NE, COLS), F32),
            pltpu.VMEM((2, 4), jnp.int32),
            pltpu.VMEM((D, 2, HID), BF16),
            pltpu.VMEM((2, D, HID), BF16),
            pltpu.VMEM((HID, D), BF16),
            pltpu.VMEM((8, HD), F32),
            pltpu.VMEM((HALF, 8, HD), F32),
            pltpu.VMEM((NE, HALF, COLS), BF16),
            pltpu.VMEM((NT, HALF, COLS), BF16),
            pltpu.VMEM((NA, NT, HALF, COLS), BF16),
            pltpu.VMEM((8, 128), F32),
            pltpu.VMEM((NA, 8, 128), F32),
            pltpu.VMEM((NT, 8, 128), F32),
            pltpu.VMEM((2 * HALF, HID), BF16),
            pltpu.VMEM((NT, NA, HALF, COLS), BF16),
            pltpu.VMEM((NA, HALF, COLS), BF16),
            pltpu.VMEM((NA, HALF, COLS), BF16),
            pltpu.VMEM((NA, HALF, COLS), BF16),
            pltpu.VMEM((4, 4, COLS), F32),
            pltpu.VMEM((NE, 4, COLS), F32),
            dma((10,)),
            dma, dma, dma, dma, dma, dma((NA,)), dma, dma((NA,)), dma, dma,
            dma((2,)), dma((2,)), dma, dma((4,)), dma, dma, dma, dma,
        ],
        compiler_params=pltpu.CompilerParams(
            collective_id=0, has_side_effects=True, vmem_limit_bytes=63 << 20
        ),
    )(
        tokens,
        queries.reshape(GROUP, HD),
        key_cache.reshape(CACHE, HD),
        value_cache.reshape(CACHE, HD),
        lengths,
        out_weight,
        norm_gain,
        router_weight.T,
        routes.T,
        up_weight.reshape(D, 2, HID),
        down_weight.reshape(HID, D),
    )


def solution(mesh):
    placed = (
        P("expert", "attn"),
        P(("attn", "tp"), "expert", None),
        P(("attn", "tp"), "expert", None, None),
        P(("attn", "tp"), "expert", None, None),
        P(("attn", "tp")),
        P("expert", "attn"),
        P("attn"),
        P("attn", None),
        P("expert", None),
        P("expert", None, None, ("attn", "tp")),
        P("expert", ("attn", "tp"), None),
    )
    return jax.shard_map(
        shards, mesh=mesh, in_specs=placed, out_specs=P("expert", "attn"), check_vma=False
    )
```

```python
import jax
import jax.numpy as jnp
from jax import lax
from jax.experimental import pallas as pl
from jax.experimental.pallas import tpu as pltpu
from jax.sharding import PartitionSpec as P

MESH = pl.DeviceIdType.MESH
F32, BF16 = jnp.float32, jnp.bfloat16
D = 6144
HD = 128
GROUP = 6
CACHE = 4096
NA, NE, NT = 16, 8, 2
HALF = 16
COLS = 384
HID = 256
NEAR = sorted(
    ((dy, dx) for dy in range(4) for dx in range(4)),
    key=lambda o: min(o[0], 4 - o[0]) + min(o[1], 4 - o[1]),
)


def drain(ref, sem):
    pltpu.make_async_copy(ref, ref, sem).wait()


def kernel(
    tok_hbm, q_hbm, k_hbm, v_hbm, len_ref, wo_hbm, gain_hbm, router_hbm, routes_hbm, up_hbm, down_hbm,
    out_ref,
    tok, q, k, v, wo, gain, router, routes, up, up2, down,
    heads, gath, zsum, resid, feats, stat, stats, logit_half, reduced, back, ret_s, ret,
    in_sem, p1_s, p1_r, p2_s, p2_r, p3_s, p3_r, st_s, st_r, sib_s, sib_r, w_s, w_r, dn_s, dn_r, p4_s, p4_r, p5_s, p5_r,
):
    a, e, t = lax.axis_index("attn"), lax.axis_index("expert"), lax.axis_index("tp")
    ay, ax = lax.div(a, 4), lax.rem(a, 4)
    sib = (a, e, 1 - t)

    def near(o):
        return lax.rem(ay + o[0], 4) * 4 + lax.rem(ax + o[1], 4)

    loads = {}
    pairs = (
        ("q", q_hbm, q), ("k", k_hbm, k), ("v", v_hbm, v), ("wo", wo_hbm, wo), ("tok", tok_hbm, tok),
        ("gain", gain_hbm, gain), ("router", router_hbm, router), ("routes", routes_hbm, routes),
        ("up", up_hbm, up), ("down", down_hbm, down.at[0]),
    )
    for n, (name, src, dst) in enumerate(pairs):
        loads[name] = pltpu.make_async_copy(src, dst, in_sem.at[n])
        loads[name].start()

    barrier = pltpu.get_barrier_semaphore()

    def greet_plane(j, c):
        other = lax.rem(2 * a + t + 1 + j, 32)
        pl.semaphore_signal(
            barrier, inc=1, device_id=(lax.div(other, 2), e, lax.rem(other, 2)), device_id_type=MESH
        )
        return c

    def greet_z(j, c):
        other = lax.rem(2 * e + t + 2 + j, 16)
        pl.semaphore_signal(
            barrier, inc=1, device_id=(a, lax.rem(e + 1 + lax.div(j, 2), NE), lax.rem(other, 2)), device_id_type=MESH
        )
        return c

    lax.fori_loop(0, 31, greet_plane, 0)
    lax.fori_loop(0, 14, greet_z, 0)

    loads["q"].wait()
    loads["k"].wait()
    scores = lax.dot_general(
        q[...], k[...], (((1,), (1,)), ((), ())), preferred_element_type=F32
    ) * (HD**-0.5)
    live = lax.broadcasted_iota(jnp.int32, scores.shape, 1) < len_ref[0]
    scores = jnp.where(live, scores, -jnp.inf)
    weights = jnp.exp(scores - jnp.max(scores, axis=1, keepdims=True))
    total = jnp.sum(weights, axis=1, keepdims=True)
    probs = (weights / total).astype(BF16)
    loads["v"].wait()
    mixed = jnp.dot(probs, v[...], preferred_element_type=F32)
    heads[...] = jnp.zeros_like(heads)
    heads[0:GROUP, :] = mixed

    pl.semaphore_wait(barrier, 45)

    half = lax.div(a, 8)
    slot = 2 * lax.rem(a, 8) + t

    def send_heads(o):
        pltpu.make_async_remote_copy(
            src_ref=heads, dst_ref=gath.at[slot], send_sem=p1_s, recv_sem=p1_r,
            device_id=(near(o), e, half), device_id_type=MESH,
        ).start()

    for o in NEAR[:0:-1]:
        send_heads(o)

    @pl.when(half != t)
    def _():
        send_heads((0, 0))

    @pl.when(half == t)
    def _():
        gath[slot] = heads[...]

    loads["up"].wait()

    def relayout(i, c):
        s = pl.ds(pl.multiple_of(i * COLS, COLS), COLS)
        up2[0:2, s, :] = jnp.swapaxes(up[s].astype(F32), 0, 1).astype(BF16)
        pltpu.make_async_remote_copy(
            src_ref=up2.at[pl.ds(0, 2), s], dst_ref=up2.at[pl.ds(2, 2), s], send_sem=w_s, recv_sem=w_r.at[i],
            device_id=sib, device_id_type=MESH,
        ).start()
        return c

    lax.fori_loop(0, D // COLS, relayout, 0)
    for name in ("wo", "tok", "gain", "router", "routes", "down"):
        loads[name].wait()
    mine = lax.broadcasted_iota(jnp.int32, (HALF, COLS), 0) // 4 == e - 4 * t
    tokens = jnp.where(mine, jnp.concatenate([tok[...].astype(F32)] * 4, axis=0), 0.0)

    @pl.when(half == t)
    def _():
        drain(gath.at[pl.ds(0, 15)], p1_r)

    @pl.when(half != t)
    def _():
        drain(gath, p1_r)

    flat = jnp.concatenate([gath[:, h, :].astype(BF16) for h in range(GROUP)], axis=1)
    projected = jnp.dot(flat, wo[...], preferred_element_type=F32) + tokens
    zsum[e] = projected.astype(BF16)

    for dz in (4, 3, 5, 2, 6, 1, 7):
        pltpu.make_async_remote_copy(
            src_ref=zsum.at[e], dst_ref=zsum.at[e], send_sem=p2_s, recv_sem=p2_r,
            device_id=(a, lax.rem(e + dz, NE), t), device_id_type=MESH,
        ).start()
    down_copy = pltpu.make_async_remote_copy(
        src_ref=down.at[0], dst_ref=down.at[1], send_sem=dn_s, recv_sem=dn_r, device_id=sib, device_id_type=MESH
    )
    down_copy.start()
    gains = gain[...].reshape(1, COLS).astype(F32)
    drain(zsum.at[pl.ds(0, 7)], p2_r)
    rounded = sum(zsum[i].astype(F32) for i in range(NE)).astype(BF16)
    wide = rounded.astype(F32)
    gained = wide * gains
    feats[a] = gained.astype(BF16)

    def feature_copy(o):
        return pltpu.make_async_remote_copy(
            src_ref=feats.at[a], dst_ref=feats.at[a], send_sem=p3_s, recv_sem=p3_r.at[a],
            device_id=(near(o), e, t), device_id_type=MESH,
        )

    for o in NEAR[:0:-1]:
        feature_copy(o).start()
    resid[t] = rounded
    resid_copy = pltpu.make_async_remote_copy(
        src_ref=resid.at[t], dst_ref=resid.at[t], send_sem=sib_s.at[0], recv_sem=sib_r.at[0],
        device_id=sib, device_id_type=MESH,
    )
    resid_copy.start()

    lane = lax.broadcasted_iota(jnp.int32, (HALF, 128), 1)
    table = jnp.where(lane == 8, jnp.sum(wide * wide, axis=1, keepdims=True), 0.0)
    for x in range(NE):
        table = table + jnp.where(
            lane == x, jnp.sum(gained * router[x : x + 1, :], axis=1, keepdims=True), 0.0
        )
    stat[...] = table[0:8] + pltpu.roll(table[8:16], 64, 1)
    for o in NEAR[:0:-1]:
        pltpu.make_async_remote_copy(
            src_ref=stat, dst_ref=stats.at[a], send_sem=st_s, recv_sem=st_r,
            device_id=(near(o), e, t), device_id_type=MESH,
        ).start()
    stats[a] = stat[...]

    accs = [jnp.zeros((HALF, HID), F32)] * 4
    for j, o in enumerate(NEAR):
        b = near(o)
        if j > 0:
            drain(feats.at[b], p3_r.at[b])
        s = pl.ds(pl.multiple_of(b * COLS, COLS), COLS)
        drain(up2.at[pl.ds(2, 2), s], w_r.at[b])
        x = feats[b]
        accs = [acc + jnp.dot(x, up2[i, s, :], preferred_element_type=F32) for i, acc in enumerate(accs)]
    drain(stats.at[pl.ds(0, 15)], st_r)
    total_stat = sum(stats[i] for i in range(NA))
    tots = jnp.concatenate([total_stat, pltpu.roll(total_stat, 64, 1)], axis=0)
    scale = lax.rsqrt(tots[:, 8:9] / D + 1e-05)
    accs = [acc * scale for acc in accs]
    hidden = [(accs[i] * jax.nn.sigmoid(accs[i]) * accs[i + 1]).astype(BF16) for i in (0, 2)]
    logit_half[t] = tots * scale
    logit_copy = pltpu.make_async_remote_copy(
        src_ref=logit_half.at[t], dst_ref=logit_half.at[t], send_sem=sib_s.at[1], recv_sem=sib_r.at[1],
        device_id=sib, device_id_type=MESH,
    )

    down_copy.wait_recv()
    for g in (2, 1, 3, 0):
        c = lax.rem(ay + g, 4)
        s = pl.ds(pl.multiple_of(c * (4 * COLS), 4 * COLS), 4 * COLS)
        d = sum(jnp.dot(hidden[i], down[i, :, s], preferred_element_type=F32) for i in range(2)).astype(BF16)
        for i in range(4):
            reduced[4 * c + i] = d[:, i * COLS : (i + 1) * COLS]
        for i in (2, 1, 3, 0):
            b = 4 * c + lax.rem(ax + i, 4)
            if (g, i) != (0, 0):
                pltpu.make_async_remote_copy(
                    src_ref=reduced.at[b], dst_ref=back.at[a], send_sem=p4_s, recv_sem=p4_r,
                    device_id=(b, e, t), device_id_type=MESH,
                ).start()
    back[a] = reduced[a]
    logit_copy.start()

    drain(logit_half.at[1 - t], sib_r.at[1])
    own = sum(
        jnp.where(e == 4 * h + i, logit_half[h, 4 * i : 4 * i + 4, :], 0.0) for h in range(2) for i in range(4)
    )
    square = (4, 128)
    lanes = lax.broadcasted_iota(jnp.int32, square, 1)
    rows = lax.broadcasted_iota(jnp.int32, (4, 4), 0)
    diag = lax.broadcasted_iota(jnp.int32, (4, 4), 1) == rows
    names = [
        jnp.sum(jnp.where(diag, jnp.broadcast_to(routes[n : n + 1, :], (4, 4)), 0), axis=1, keepdims=True)
        for n in range(2)
    ]
    chosen = [jnp.sum(jnp.where(lanes == names[n], own, 0.0), axis=1, keepdims=True) for n in range(2)]
    gates = [jax.nn.sigmoid(chosen[0] - chosen[1]), jax.nn.sigmoid(chosen[1] - chosen[0])]
    drain(resid.at[1 - t], sib_r.at[0])
    base = jnp.zeros((4, COLS), F32)
    for h in range(2):
        both = resid[h].astype(F32)
        for i in range(4):
            base = base + jnp.where(e == 4 * h + i, both[4 * i : 4 * i + 4], 0.0)

    drain(back.at[pl.ds(0, 15)], p4_r)
    summed = sum(back[i].astype(F32) for i in range(NA))

    for i in range(4):
        ret_s[i] = summed[4 * i : 4 * i + 4]
    for i in range(4):
        for other in range(2):
            row_owner = 4 * t + i
            itself = jnp.logical_and(row_owner == e, other == t)

            @pl.when(jnp.logical_not(itself))
            def _():
                pltpu.make_async_remote_copy(
                    src_ref=ret_s.at[i], dst_ref=ret.at[e], send_sem=p5_s, recv_sem=p5_r,
                    device_id=(a, row_owner, other), device_id_type=MESH,
                ).start()

            @pl.when(itself)
            def _():
                ret[e] = ret_s[i]

    home = lax.div(e, 4) == t

    @pl.when(home)
    def _():
        drain(ret.at[pl.ds(0, 7)], p5_r)
        drain(ret.at[pl.ds(0, 7)], p5_s)

    @pl.when(jnp.logical_not(home))
    def _():
        drain(ret, p5_r)
        drain(ret, p5_s)

    for x in range(NE):
        share = sum(jnp.where(names[n] == x, gates[n], 0.0) for n in range(2))
        base = base + share * ret[x]
    out_ref[...] = base.astype(BF16)

    @pl.when(half == t)
    def _():
        drain(gath.at[pl.ds(0, 15)], p1_s)

    @pl.when(half != t)
    def _():
        drain(gath, p1_s)

    drain(zsum.at[pl.ds(0, 7)], p2_s)
    drain(back.at[pl.ds(0, 15)], p3_s)
    drain(stats.at[pl.ds(0, 15)], st_s)
    drain(resid.at[t], sib_s.at[0])
    drain(logit_half.at[t], sib_s.at[1])
    drain(up2.at[pl.ds(0, 2)], w_s)
    down_copy.wait_send()
    drain(back.at[pl.ds(0, 15)], p4_s)


def shards(
    tokens, queries, key_cache, value_cache, lengths, out_weight, norm_gain, router_weight, routes, up_weight, down_weight
):
    hbm = pl.BlockSpec(memory_space=pl.ANY)
    dma = pltpu.SemaphoreType.DMA
    return pl.pallas_call(
        kernel,
        out_shape=jax.ShapeDtypeStruct((4, COLS), BF16),
        in_specs=[hbm] * 4 + [pl.BlockSpec(memory_space=pltpu.SMEM)] + [hbm] * 6,
        out_specs=pl.BlockSpec(memory_space=pltpu.VMEM),
        scratch_shapes=[
            pltpu.VMEM((4, COLS), BF16),
            pltpu.VMEM((GROUP, HD), BF16),
            pltpu.VMEM((CACHE, HD), BF16),
            pltpu.VMEM((CACHE, HD), BF16),
            pltpu.VMEM((GROUP * HD, COLS), BF16),
            pltpu.VMEM((COLS,), BF16),
            pltpu.VMEM((NE, COLS), F32),
            pltpu.VMEM((2, 4), jnp.int32),
            pltpu.VMEM((D, 2, HID), BF16),
            pltpu.VMEM((4, D, HID), BF16),
            pltpu.VMEM((2, HID, D), BF16),
            pltpu.VMEM((8, HD), F32),
            pltpu.VMEM((HALF, 8, HD), F32),
            pltpu.VMEM((NE, HALF, COLS), BF16),
            pltpu.VMEM((NT, HALF, COLS), BF16),
            pltpu.VMEM((NA, HALF, COLS), BF16),
            pltpu.VMEM((8, 128), F32),
            pltpu.VMEM((NA, 8, 128), F32),
            pltpu.VMEM((NT, HALF, 128), F32),
            pltpu.VMEM((NA, HALF, COLS), BF16),
            pltpu.VMEM((NA, HALF, COLS), BF16),
            pltpu.VMEM((4, 4, COLS), F32),
            pltpu.VMEM((NE, 4, COLS), F32),
            dma((10,)),
            dma, dma, dma, dma, dma, dma((NA,)), dma, dma, dma((2,)), dma((2,)),
            dma, dma((NA,)), dma, dma, dma, dma, dma, dma,
        ],
        compiler_params=pltpu.CompilerParams(
            collective_id=0, has_side_effects=True, vmem_limit_bytes=63 << 20
        ),
    )(
        tokens,
        queries.reshape(GROUP, HD),
        key_cache.reshape(CACHE, HD),
        value_cache.reshape(CACHE, HD),
        lengths,
        out_weight,
        norm_gain,
        router_weight.T,
        routes.T,
        up_weight.reshape(D, 2, HID),
        down_weight.reshape(HID, D),
    )


def solution(mesh):
    placed = (
        P("expert", "attn"),
        P(("attn", "tp"), "expert", None),
        P(("attn", "tp"), "expert", None, None),
        P(("attn", "tp"), "expert", None, None),
        P(("attn", "tp")),
        P("expert", "attn"),
        P("attn"),
        P("attn", None),
        P("expert", None),
        P("expert", None, None, ("attn", "tp")),
        P("expert", ("attn", "tp"), None),
    )
    return jax.shard_map(
        shards, mesh=mesh, in_specs=placed, out_specs=P("expert", "attn"), check_vma=False
    )
```
